32 devices in a mesh: groups: 2 (over y), job: 4 (over x, core), tensor: 4 (over z).
Axes of the slice: x: 2, y: 2, z: 4, core: 2. Of those that a mesh axis runs over, the one named last changes fastest.
Arguments:
- tokens: bfloat16 [12288, 8192], P(('groups', 'job'), 'tensor'), parts along dimension 0, may hold values from -6 to 6
- frozen_key_weight: bfloat16 [8192, 1024], P('tensor'), may hold values from -0.0625 to 0.0625
- adapter_down_maps: bfloat16 [32, 8192, 64], P('job', 'tensor'), may hold values from -0.0625 to 0.0625
- adapter_up_maps: bfloat16 [32, 64, 1024], P('job', 'tensor'), may hold values from -0.75 to 0.75
- cotangent: bfloat16 [12288, 1024], P(('groups', 'job', 'tensor')), parts along dimension 0, may hold values from -6 to 6
- block_owner_job: int32 [96, 1], P('groups'), parts along dimension 0, may hold values from 0 to 3; in each aligned block of 12 rows (0 to 11, 12 to 23, ...) at most 4 rows name the same one
- block_local_adapter: int32 [96], P('groups'), parts along dimension 0, may hold values from 0 to 7
- block_live_rows: int32 [96], P('groups'), parts along dimension 0, may hold values from 0 to 128
Outputs:
- projected: bfloat16 [12288, 1024], P(('groups', 'job', 'tensor')), parts along dimension 0
- grad_tokens: bfloat16 [12288, 8192], P(('groups', 'job'), 'tensor'), parts along dimension 0
- grad_down: float32 [64, 8192, 64], P(('groups', 'job'), 'tensor'), parts along dimension 0
- grad_up: float32 [64, 64, 1024], P(('groups', 'job'), 'tensor'), parts along dimension 0
The draws below stay inside these ranges and needn't reach their ends.
There are 2 independent parts, one for each index of `groups`. The reference program is written for one: setup_inputs(seed, part) draws one part's arguments, and reference() takes and returns one part's arrays. A program takes and returns all parts, laid end to end along the dimension named above; an argument that names none is the same for every part. Nothing has to cross between parts.
Inputs may be any that keep to these rules, and one draw needn't show every extreme that they name: `block_owner_job`: in each aligned run of 12 blocks (the slots of one index of job), at most 4 blocks name the same owner.
All inputs are finite; a program needn't handle non-finite values.
Results may differ from the reference program's by a relative error of at most 0.015.
Values may be sent and summed in bfloat16 or wider, within the bound.
A program may use at most 128 MiB of HBM per device.

```python
import math
import jax
import jax.numpy as jnp
import numpy as np
from jax import lax

MODEL_WIDTH = 8192
KEY_WIDTH = 1024
ADAPTER_RANK = 64
BLOCK = 128
ADAPTERS_DEV = 8
BLOCKS_DEV = 12
SLOT_CAP = 4
ADAPTER_TOTAL = 32
BLOCKS = 48
ROWS = 6144
D_PART = 2048
R_PART = 16
N_JOB = 4
N_TENSOR = 4


def with_ends(array, key, low, top_value):
    spot = [jax.random.randint(jax.random.fold_in(key, axis), (), 0, length) for axis, length in enumerate(array.shape)]
    longest = array.shape.index(max(array.shape))
    neighbour = spot[:longest] + [(spot[longest] + 1) % array.shape[longest]] + spot[longest + 1:]
    return array.at[tuple(spot)].set(low).at[tuple(neighbour)].set(top_value)


def steps_of(stream_key, extent, pieces, smallest, largest):
    def one(position, parts):
        steps = jax.random.uniform(jax.random.fold_in(jax.random.fold_in(stream_key, 6), position), (parts,), jnp.float32, smallest / len(pieces), largest / len(pieces))
        return jnp.repeat(jnp.exp(steps), extent[position] // parts).reshape((-1,) + (1,) * (len(extent) - position - 1))

    loudness = one(*pieces[0])
    for cut in pieces[1:]:
        loudness = loudness * one(*cut)
    return loudness


def deal_out(stream_key, own, number, rows, count, top, reach, slope):
    sequence = jax.random.permutation(stream_key, count)
    crowded, ordinary = shares(count, rows * top, reach, slope, True), shares(count, rows * top, reach, slope, False)
    places = jnp.arange(count)

    def named(tallies, rotation):
        used = int((tallies > 0).sum())
        fixed = max(1, used // 4)
        passed = fixed + (places - fixed + rotation * (used - fixed)) % max(1, count - fixed)
        return jnp.zeros((count,), jnp.int32).at[sequence[jnp.where(places < fixed, places, passed)]].set(jnp.asarray(tallies, jnp.int32))

    tallies = jnp.where(number % 4 == 0, named(crowded, number // 4), named(ordinary, number - number // 4 - 1))
    mixed = jax.random.permutation(jax.random.fold_in(own, 3), count)
    giver, sink = mixed[0:count // 2 * 2:2], mixed[1:count // 2 * 2:2]
    room = jnp.minimum(tallies[giver] - 1, reach - tallies[sink]) // 2
    room = jnp.where((giver == sequence[0]) | (sink == sequence[0]) | (tallies[sink] == 0), 0, jnp.maximum(room, 0))
    passed = jax.random.randint(jax.random.fold_in(own, 4), (count // 2,), 0, 1 << 20) % (room + 1)
    tallies = tallies.at[giver].add(-passed).at[sink].add(passed)
    items = jnp.searchsorted(jnp.cumsum(tallies), jnp.arange(rows * top), side="right").astype(jnp.int32)
    table = items.reshape(top, rows).T
    table = table[jax.random.permutation(jax.random.fold_in(own, 1), rows)]
    rotation = jax.random.randint(jax.random.fold_in(own, 2), (rows, 1), 0, top)
    return jnp.take_along_axis(table, (jnp.arange(top)[None, :] + rotation) % top, axis=1)


def shares(count, total, reach, lean, full):
    weights = [(1 << 20) // math.isqrt(grade ** lean) + 1 for grade in range(1, count + 1)]
    largest = reach if full else min(reach, max(-(-total // count), total * weights[0] // sum(weights)))
    least = 1 if total - largest >= count - 1 else 0
    given, spare = [largest] + [least] * (count - 1), total - largest - least * (count - 1)
    while spare > 0:
        candidates = [i for i in range(1, count) if given[i] < largest] or [i for i in range(1, count) if given[i] < reach]
        mass, budget = sum([weights[i] for i in candidates]), spare
        for i in candidates:
            addition = min(reach - given[i], max(1, budget * weights[i] // mass), spare)
            given[i] = given[i] + addition
            spare = spare - addition
    return np.array(given)


def scatter_about(rng, dims, deviation, most, split=(), kind=jnp.bfloat16):
    drawn = jax.random.normal(rng, dims, jnp.float32) * deviation
    if len(split) > 0:
        drawn = steps_of(rng, dims, split, -0.22, 0.18) * drawn
    return jnp.clip(drawn, min=-most, max=most).astype(kind)


def setup_inputs(seed: int = 0, part: int = 0) -> dict:
    splits = jax.random.split(jax.random.key(seed), 9)
    own_keys = jax.random.split(jax.random.fold_in(splits[8], part), 9)
    tokens = scatter_about(own_keys[0], (ROWS, MODEL_WIDTH), 1.0, 6.0, ((0, 4), (1, 4)))
    frozen_key_weight = scatter_about(splits[1], (MODEL_WIDTH, KEY_WIDTH), MODEL_WIDTH ** -0.5, 0.0625, ((0, 4),))
    adapter_down_maps = scatter_about(splits[2], (ADAPTER_TOTAL, MODEL_WIDTH, ADAPTER_RANK), MODEL_WIDTH ** -0.5, 0.0625, ((0, 4), (1, 4)))
    adapter_up_maps = scatter_about(splits[3], (ADAPTER_TOTAL, ADAPTER_RANK, KEY_WIDTH), ADAPTER_RANK ** -0.5, 0.75, ((0, 4), (1, 4)))
    cotangent = scatter_about(own_keys[4], (ROWS, KEY_WIDTH), 1.0, 6.0, ((0, 16),))
    block_owner_job_keys = jax.random.split(jax.random.fold_in(own_keys[5], 1), BLOCKS // BLOCKS_DEV)
    block_owner_job_turns = jax.random.permutation(jax.random.fold_in(own_keys[5], 3), BLOCKS // BLOCKS_DEV)
    block_owner_job = jax.vmap(lambda own, number: deal_out(jax.random.fold_in(own_keys[5], 2), own, number, BLOCKS_DEV, N_JOB, 1, SLOT_CAP, 2))(block_owner_job_keys, block_owner_job_turns).reshape((BLOCKS, 1))
    block_local_adapter = with_ends(jax.random.randint(own_keys[6], (BLOCKS,), 0, ADAPTERS_DEV), jax.random.fold_in(own_keys[6], 1), 0, ADAPTERS_DEV - 1).astype(jnp.int32)
    block_live_rows = with_ends(jax.random.randint(own_keys[7], (BLOCKS,), 0, BLOCK + 1), jax.random.fold_in(own_keys[7], 1), 0, BLOCK).astype(jnp.int32)
    return {"tokens": tokens, "frozen_key_weight": frozen_key_weight, "adapter_down_maps": adapter_down_maps, "adapter_up_maps": adapter_up_maps, "cotangent": cotangent, "block_owner_job": block_owner_job, "block_local_adapter": block_local_adapter, "block_live_rows": block_live_rows}


adapter_scale = 2.0


def block_rank(pair):
    return jnp.dot(pair[0], pair[1], preferred_element_type=jnp.float32)


def block_back(pair):
    return jnp.dot(pair[0], pair[1].T, preferred_element_type=jnp.float32)


def block_outer(pair):
    return jnp.dot(pair[0].T, pair[1], preferred_element_type=jnp.float32)


def reference(tokens, frozen_key_weight, adapter_down_maps, adapter_up_maps, cotangent, block_owner_job, block_local_adapter, block_live_rows):
    block_total = block_live_rows.shape[0]
    adapter_number = (ADAPTERS_DEV * block_owner_job[:, 0] + block_local_adapter).astype(jnp.int32)
    live_rows = (jnp.arange(BLOCK, dtype=jnp.int32)[None, :] < block_live_rows[:, None]).reshape(-1)
    masked = tokens * live_rows[:, None].astype(jnp.bfloat16)
    row_blocks = masked.reshape(block_total, BLOCK, MODEL_WIDTH)
    block_down_maps = jnp.take(adapter_down_maps, adapter_number, axis=0)
    up_map_wide = jnp.take(adapter_up_maps, adapter_number, axis=0).astype(jnp.float32)
    rank_row_values = lax.map(block_rank, (row_blocks, block_down_maps))

    def shard_sum(total, index):
        feature_columns = lax.dynamic_slice_in_dim(masked, index * D_PART, D_PART, 1)
        weight_row_values = lax.dynamic_slice_in_dim(frozen_key_weight, index * D_PART, D_PART, 0)
        rank_columns = lax.dynamic_slice_in_dim(rank_row_values, index * R_PART, R_PART, 2)
        up_map_rows = lax.dynamic_slice_in_dim(up_map_wide, index * R_PART, R_PART, 1)
        adapter_term = jnp.einsum("seu,sui->sei", rank_columns, up_map_rows, precision=lax.Precision.HIGHEST)
        term_value = jnp.dot(feature_columns, weight_row_values, preferred_element_type=jnp.float32) + adapter_scale * adapter_term.reshape(-1, KEY_WIDTH)
        rounded = lax.optimization_barrier(term_value.astype(jnp.bfloat16))
        return total + rounded.astype(jnp.float32), None

    projected, _ = lax.scan(shard_sum, jnp.zeros((masked.shape[0], KEY_WIDTH), jnp.float32), jnp.arange(N_TENSOR, dtype=jnp.int32))
    cotangent_blocks = cotangent.reshape(block_total, BLOCK, KEY_WIDTH).astype(jnp.float32)
    rank_gradient = (adapter_scale * jnp.einsum("ald,afd->alf", cotangent_blocks, up_map_wide, precision=lax.Precision.HIGHEST)).astype(jnp.bfloat16)
    grad_rows = jnp.dot(cotangent, frozen_key_weight.T, preferred_element_type=jnp.float32)
    grad_rows = grad_rows + lax.map(block_back, (rank_gradient, block_down_maps)).reshape(-1, MODEL_WIDTH)
    grad_tokens = (grad_rows * live_rows[:, None].astype(jnp.float32)).astype(jnp.bfloat16)
    down_terms = lax.map(block_outer, (row_blocks, rank_gradient))
    grad_down = jax.ops.segment_sum(down_terms, adapter_number, num_segments=ADAPTER_TOTAL)
    up_map_terms = adapter_scale * jnp.einsum("xhw,xhk->xwk", rank_row_values, cotangent_blocks, precision=lax.Precision.HIGHEST)
    grad_up = jax.ops.segment_sum(up_map_terms, adapter_number, num_segments=ADAPTER_TOTAL)
    return projected.astype(jnp.bfloat16), grad_tokens, grad_down, grad_up
```

```python
import functools

import jax
import jax.numpy as jnp
from jax import lax
from jax.experimental import pallas as pl
from jax.experimental.pallas import tpu as pltpu
from jax.sharding import PartitionSpec as P

BLOCK = 128
SLOT_CAP = 4
VMEM_LIMIT = 48 * 1024 * 1024


adapter_scale = 2.0

NT = (((1,), (1,)), ((), ()))
TN = (((0,), (0,)), ((), ()))


def dot(a, b, dims):
    return lax.dot_general(a, b, dims, preferred_element_type=jnp.float32)


def general(
    tokens,
    frozen_key_weight,
    adapter_down_maps,
    adapter_up_maps,
    cotangent,
    block_owner_job,
    block_local_adapter,
    block_live_rows,
):
    job_count = lax.axis_size("job")
    own_job = lax.axis_index("job")
    row_total = tokens.shape[0]
    block_count = row_total // BLOCK
    local_adapters = adapter_down_maps.shape[0]
    width_portion = adapter_down_maps.shape[1]
    full_rank_values = adapter_down_maps.shape[2]
    rank_portion = adapter_up_maps.shape[1]
    output_width = adapter_up_maps.shape[2]
    owners_all = block_owner_job[:, 0].reshape(job_count, block_count)
    locals_all = block_local_adapter.reshape(job_count, block_count)
    fills_all = block_live_rows.reshape(job_count, block_count)
    my_owner = lax.dynamic_index_in_dim(owners_all, own_job, 0, keepdims=False)
    my_local = lax.dynamic_index_in_dim(locals_all, own_job, 0, keepdims=False)
    my_fill = lax.dynamic_index_in_dim(fills_all, own_job, 0, keepdims=False)
    adapter_ids = my_owner * local_adapters + my_local
    live_rows = (jnp.arange(BLOCK, dtype=jnp.int32)[None, :] < my_fill[:, None]).reshape(row_total)
    masked = tokens * live_rows[:, None].astype(jnp.bfloat16)
    row_blocks = masked.reshape(block_count, BLOCK, width_portion)
    every_down, every_up = (
        lax.all_gather(adapter_down_maps, "job", axis=0, tiled=True),
        lax.all_gather(adapter_up_maps, "job", axis=0, tiled=True),
    )
    block_down_maps = jnp.take(every_down, adapter_ids, axis=0)
    up_blocks = jnp.take(every_up, adapter_ids, axis=0)
    rank_terms = jnp.einsum(
        "bnd,bdr->bnr", row_blocks, block_down_maps, preferred_element_type=jnp.float32
    ).reshape(row_total, full_rank_values)
    rank_mine = lax.psum_scatter(
        rank_terms.astype(jnp.bfloat16), "tensor", scatter_dimension=1, tiled=True
    ).astype(jnp.float32)
    rank_blocks = rank_mine.reshape(block_count, BLOCK, rank_portion)
    adapter_rows = jnp.einsum(
        "seu,sui->sei", rank_blocks, up_blocks.astype(jnp.float32), precision=lax.Precision.HIGHEST
    ).reshape(row_total, output_width)
    projected = lax.psum_scatter(
        (
            jnp.dot(masked, frozen_key_weight, preferred_element_type=jnp.float32)
            + adapter_scale * adapter_rows
        ).astype(jnp.bfloat16),
        "tensor",
        scatter_dimension=0,
        tiled=True,
    )
    grad_full = lax.all_gather(cotangent, "tensor", axis=0, tiled=True)
    grad_blocks = grad_full.reshape(block_count, BLOCK, output_width)
    rank_grad_mine = (
        adapter_scale
        * jnp.einsum("ald,afd->alf", grad_blocks, up_blocks, preferred_element_type=jnp.float32)
    ).astype(jnp.bfloat16)
    rank_grad_all = lax.all_gather(
        rank_grad_mine.reshape(row_total, rank_portion), "tensor", axis=1, tiled=True
    )
    rank_grad_blocks = rank_grad_all.reshape(block_count, BLOCK, full_rank_values)
    grad_rows = lax.dot_general(
        grad_full, frozen_key_weight, (((1,), (1,)), ((), ())), preferred_element_type=jnp.float32
    )
    grad_rows = grad_rows + jnp.einsum(
        "bnr,bdr->bnd", rank_grad_blocks, block_down_maps, preferred_element_type=jnp.float32
    ).reshape(row_total, width_portion)
    grad_tokens = (grad_rows * live_rows[:, None].astype(jnp.float32)).astype(jnp.bfloat16)
    down_terms = jnp.einsum(
        "bnd,bnr->bdr", row_blocks, rank_grad_blocks, preferred_element_type=jnp.float32
    ).reshape(block_count, -1)
    up_map_terms = (
        adapter_scale
        * jnp.einsum(
            "xhw,xhk->xwk",
            rank_blocks,
            grad_blocks.astype(jnp.float32),
            precision=lax.Precision.HIGHEST,
        )
    ).reshape(block_count, -1)
    adapter_range = jnp.arange(job_count * local_adapters, dtype=jnp.int32)
    onehot = (adapter_ids[None, :] == adapter_range[:, None]).astype(jnp.float32)
    dense_down = jnp.einsum(
        "ab,bx->ax", onehot, down_terms, precision=lax.Precision.HIGHEST
    ).reshape(job_count, local_adapters, -1)
    dense_up = jnp.einsum(
        "ab,bx->ax", onehot, up_map_terms, precision=lax.Precision.HIGHEST
    ).reshape(job_count, local_adapters, -1)
    got_down, got_up = (
        lax.all_to_all(
            dense_down.astype(jnp.bfloat16), "job", split_axis=0, concat_axis=0, tiled=True
        ).astype(dense_down.dtype),
        lax.all_to_all(
            dense_up.astype(jnp.bfloat16), "job", split_axis=0, concat_axis=0, tiled=True
        ).astype(dense_up.dtype),
    )
    grad_down = jnp.sum(got_down, axis=0)
    grad_up = jnp.sum(got_up, axis=0)
    grad_down = grad_down.reshape(local_adapters, width_portion, full_rank_values)
    grad_up = grad_up.reshape(local_adapters, rank_portion, output_width)
    return (projected, grad_tokens, grad_down, grad_up)


def rank_kernel(slot_ref, tokens_ref, down_ref, live_ref, out_ref):
    block_rank = dot(down_ref[0], tokens_ref[...], NT)
    out_ref[0] = (block_rank * live_ref[0]).astype(out_ref.dtype)


def rank_partials(tokens, got_down, my_slot, live):
    row_total, width = tokens.shape
    block_count = row_total // BLOCK
    rank = got_down.shape[1]
    return pl.pallas_call(
        rank_kernel,
        grid_spec=pltpu.PrefetchScalarGridSpec(
            num_scalar_prefetch=1,
            grid=(block_count,),
            in_specs=[
                pl.BlockSpec((BLOCK, width), lambda b, slot: (b, 0)),
                pl.BlockSpec((1, rank, width), lambda b, slot: (slot[b], 0, 0)),
                pl.BlockSpec((1, 1, BLOCK), lambda b, slot: (b, 0, 0)),
            ],
            out_specs=pl.BlockSpec((1, rank, BLOCK), lambda b, slot: (b, 0, 0)),
        ),
        out_shape=jax.ShapeDtypeStruct((block_count, rank, BLOCK), jnp.bfloat16),
        compiler_params=pltpu.CompilerParams(vmem_limit_bytes=VMEM_LIMIT),
        cost_estimate=pl.CostEstimate(
            flops=2 * row_total * width * rank,
            bytes_accessed=2 * (row_total * width + block_count * rank * width),
            transcendentals=0,
        ),
        name="rank_partials",
    )(my_slot, tokens, got_down, live)


def grad_tokens_kernel(per_step, slot_ref, cot_ref, weight_ref, rank_grad_ref, live_ref, *rest):
    down_refs, out_ref = rest[:per_step], rest[per_step]
    for k in range(per_step):
        rows = pl.ds(k * BLOCK, BLOCK)
        total = dot(cot_ref[rows, :], weight_ref[...], NT)
        total = total + dot(rank_grad_ref[k], down_refs[k][0], TN)
        out_ref[rows, :] = (total * live_ref[rows, :]).astype(out_ref.dtype)


def token_grads(cot_full, weight, rank_grad, live_rows, got_down, my_slot, per_step):
    row_total, key_width = cot_full.shape
    width = weight.shape[0]
    rank = got_down.shape[1]
    step_rows = per_step * BLOCK
    return pl.pallas_call(
        functools.partial(grad_tokens_kernel, per_step),
        grid_spec=pltpu.PrefetchScalarGridSpec(
            num_scalar_prefetch=1,
            grid=(row_total // step_rows,),
            in_specs=[
                pl.BlockSpec((step_rows, key_width), lambda i, slot: (i, 0)),
                pl.BlockSpec((width, key_width), lambda i, slot: (0, 0)),
                pl.BlockSpec((per_step, rank, BLOCK), lambda i, slot: (i, 0, 0)),
                pl.BlockSpec((step_rows, 1), lambda i, slot: (i, 0)),
            ]
            + [
                pl.BlockSpec(
                    (1, rank, width),
                    functools.partial(lambda k, i, slot: (slot[i * per_step + k], 0, 0), k),
                )
                for k in range(per_step)
            ],
            out_specs=pl.BlockSpec((step_rows, width), lambda i, slot: (i, 0)),
        ),
        out_shape=jax.ShapeDtypeStruct((row_total, width), jnp.bfloat16),
        compiler_params=pltpu.CompilerParams(vmem_limit_bytes=VMEM_LIMIT),
        cost_estimate=pl.CostEstimate(
            flops=2 * row_total * width * (key_width + rank),
            bytes_accessed=2 * (row_total * (width + key_width) + width * key_width),
            transcendentals=0,
        ),
        name="token_grads",
    )(my_slot, cot_full, weight, rank_grad, live_rows, *([got_down] * per_step))


def down_terms_kernel(block_ref, valid_ref, tokens_ref, rank_grad_ref, out_ref):
    step = pl.program_id(0)

    @pl.when(valid_ref[step] > 0)
    def _():
        out_ref[0] = dot(rank_grad_ref[0], tokens_ref[...], (((1,), (0,)), ((), ()))).astype(
            out_ref.dtype
        )

    @pl.when(valid_ref[step] == 0)
    def _():
        out_ref[...] = jnp.zeros_like(out_ref)


def down_terms(tokens, rank_grad_live, slot_block, slot_valid):
    width = tokens.shape[1]
    slots = slot_block.shape[0]
    rank = rank_grad_live.shape[1]
    return pl.pallas_call(
        down_terms_kernel,
        grid_spec=pltpu.PrefetchScalarGridSpec(
            num_scalar_prefetch=2,
            grid=(slots,),
            in_specs=[
                pl.BlockSpec((BLOCK, width), lambda s, block, valid: (block[s], 0)),
                pl.BlockSpec((1, rank, BLOCK), lambda s, block, valid: (block[s], 0, 0)),
            ],
            out_specs=pl.BlockSpec((1, rank, width), lambda s, block, valid: (s, 0, 0)),
        ),
        out_shape=jax.ShapeDtypeStruct((slots, rank, width), jnp.bfloat16),
        compiler_params=pltpu.CompilerParams(vmem_limit_bytes=VMEM_LIMIT),
        cost_estimate=pl.CostEstimate(
            flops=2 * slots * BLOCK * width * rank,
            bytes_accessed=2 * slots * (BLOCK * width + rank * width),
            transcendentals=0,
        ),
        name="down_terms",
    )(slot_block, slot_valid, tokens, rank_grad_live)


def owner_sum_kernel(adapter_ref, valid_ref, got_ref, out_ref):
    out_ref[...] = jnp.zeros_like(out_ref)
    for s in range(got_ref.shape[0]):

        @pl.when(valid_ref[s] > 0)
        def _(s=s):
            a = adapter_ref[s]
            out_ref[a] = out_ref[a] + got_ref[s].astype(jnp.float32)


def owner_sum(got, slot_adapter, slot_valid, adapters, tile):
    slots, rank, width = got.shape
    return pl.pallas_call(
        owner_sum_kernel,
        grid_spec=pltpu.PrefetchScalarGridSpec(
            num_scalar_prefetch=2,
            grid=(width // tile,),
            in_specs=[pl.BlockSpec((slots, rank, tile), lambda i, a, v: (0, 0, i))],
            out_specs=pl.BlockSpec((adapters, rank, tile), lambda i, a, v: (0, 0, i)),
        ),
        out_shape=jax.ShapeDtypeStruct((adapters, rank, width), jnp.float32),
        compiler_params=pltpu.CompilerParams(vmem_limit_bytes=VMEM_LIMIT),
        cost_estimate=pl.CostEstimate(
            flops=slots * rank * width,
            bytes_accessed=2 * slots * rank * width + 4 * adapters * rank * width,
            transcendentals=0,
        ),
        name="owner_sum",
    )(slot_adapter, slot_valid, got)


def line_gather(own, me, n):
    right = [(i, i + 1) for i in range(n - 1)]
    from_left, from_right = [], []
    a = b = own
    for step in range(n - 1):
        a = lax.ppermute(a, "tensor", [p for p in right if p[0] >= step])
        b = lax.ppermute(b, "tensor", [(j, i) for i, j in right if j <= n - 1 - step])
        from_left.append(a)
        from_right.append(b)
    parts = from_left[::-1] + [own] + from_right
    rows = own.shape[0]
    return lax.dynamic_slice_in_dim(jnp.concatenate(parts, axis=0), (n - 1 - me) * rows, n * rows, 0)


def line_scatter(partial, me, n):
    rows = partial.shape[0] // n

    def piece(index):
        return lax.dynamic_slice_in_dim(partial, jnp.clip(index, 0, n - 1) * rows, rows, 0)

    mirrored = n - 1 - me
    a = b = None
    for step in range(n - 1):
        send_a = piece(n - 1 - step + me)
        send_b = piece(n - 1 - (n - 1 - step + mirrored))
        if step > 0:
            send_a = (send_a.astype(jnp.float32) + a.astype(jnp.float32)).astype(jnp.bfloat16)
            send_b = (send_b.astype(jnp.float32) + b.astype(jnp.float32)).astype(jnp.bfloat16)
        a = lax.ppermute(send_a, "tensor", [(i, i + 1) for i in range(n - 1) if i <= step])
        b = lax.ppermute(
            send_b, "tensor", [(n - 1 - i, n - 2 - i) for i in range(n - 1) if i <= step]
        )
    return piece(me).astype(jnp.float32) + a.astype(jnp.float32) + b.astype(jnp.float32)


def local(
    tokens,
    frozen_key_weight,
    adapter_down_maps,
    adapter_up_maps,
    cotangent,
    block_owner_job,
    block_local_adapter,
    block_live_rows,
):
    own_rows = cotangent.shape[0]
    if own_rows % BLOCK:
        return general(
            tokens,
            frozen_key_weight,
            adapter_down_maps,
            adapter_up_maps,
            cotangent,
            block_owner_job,
            block_local_adapter,
            block_live_rows,
        )
    n = lax.axis_size("tensor")
    me = lax.axis_index("tensor")
    job_count = lax.axis_size("job")
    own_job = lax.axis_index("job")
    row_total = tokens.shape[0]
    block_count = row_total // BLOCK
    own_blocks = own_rows // BLOCK
    adapters, width, rank = adapter_down_maps.shape
    rank_portion, key_width = adapter_up_maps.shape[1:]
    slots = job_count * SLOT_CAP

    owners = block_owner_job[:, 0].reshape(job_count, block_count)
    locals_all = block_local_adapter.reshape(job_count, block_count)
    earlier = jnp.tril(jnp.ones((block_count, block_count), jnp.int32), -1)
    place = jnp.sum((owners[:, :, None] == owners[:, None, :]) * earlier[None], axis=2)
    slot_of = owners * SLOT_CAP + place
    chosen = slot_of[:, None, :] == jnp.arange(slots, dtype=jnp.int32)[None, :, None]
    slot_valid = jnp.sum(chosen, axis=2, dtype=jnp.int32)
    slot_block = jnp.sum(chosen * jnp.arange(block_count, dtype=jnp.int32), axis=2)
    slot_adapter = jnp.sum(chosen * locals_all[:, None, :], axis=2)

    def of_job(table):
        return lax.dynamic_index_in_dim(table, own_job, 0, keepdims=False)

    def to_me(table):
        split = table.reshape(job_count, job_count, SLOT_CAP)
        return lax.dynamic_index_in_dim(split, own_job, 1, keepdims=False).reshape(slots)

    my_slot, my_block, my_valid = of_job(slot_of), of_job(slot_block), of_job(slot_valid)
    in_adapter, in_valid = to_me(slot_adapter), to_me(slot_valid)
    my_fill = of_job(block_live_rows.reshape(job_count, block_count))
    live = (jnp.arange(BLOCK, dtype=jnp.int32)[None, :] < my_fill[:, None]).astype(jnp.float32)
    live_lanes = live.reshape(block_count, 1, BLOCK)
    live_rows = live.reshape(row_total, 1)

    def exchange(x):
        shape = x.shape
        return lax.all_to_all(
            x.reshape((job_count, SLOT_CAP) + shape[1:]), "job", split_axis=0, concat_axis=0, tiled=True
        ).reshape(shape)

    def turn(x):
        return lax.all_to_all(x, "tensor", split_axis=0, concat_axis=0, tiled=True)

    down_t = jnp.transpose(adapter_down_maps, (0, 2, 1))
    got_up = exchange(jnp.take(adapter_up_maps, in_adapter, axis=0))
    got_down = exchange(jnp.take(down_t, in_adapter, axis=0))

    cot_full = line_gather(cotangent, me, n)

    up_blocks = jnp.take(got_up, my_slot, axis=0)
    up_own = turn(up_blocks.reshape(n, own_blocks, rank_portion, key_width))
    up_own = jnp.transpose(up_own, (1, 0, 2, 3)).reshape(own_blocks, rank, key_width)
    cot_own = cotangent.reshape(own_blocks, BLOCK, key_width)
    rank_grad_own = (
        adapter_scale
        * jnp.einsum("brd,bld->brl", up_own, cot_own, preferred_element_type=jnp.float32)
    ).astype(jnp.bfloat16)
    rank_grad = turn(jnp.broadcast_to(rank_grad_own[None], (n,) + rank_grad_own.shape))
    rank_grad = rank_grad.reshape(block_count, rank, BLOCK)
    rank_grad_live = rank_grad * live_lanes.astype(jnp.bfloat16)

    got_terms = exchange(down_terms(tokens, rank_grad_live, my_block, my_valid))

    partial = (
        jnp.dot(tokens, frozen_key_weight, preferred_element_type=jnp.float32) * live_rows
    ).astype(jnp.bfloat16)
    base = line_scatter(partial, me, n)

    rank_part = rank_partials(tokens, got_down, my_slot, live_lanes)
    rank_sum = jnp.sum(
        turn(rank_part.reshape(n, own_blocks, rank, BLOCK)).astype(jnp.float32), axis=0
    ).astype(jnp.bfloat16)
    adapter_rows = jnp.einsum("brl,brd->bld", rank_sum, up_own, preferred_element_type=jnp.float32)
    projected = (base + adapter_scale * adapter_rows.reshape(own_rows, key_width)).astype(
        jnp.bfloat16
    )

    rank_mine = turn(
        jnp.transpose(rank_sum.reshape(own_blocks, n, rank_portion, BLOCK), (1, 0, 2, 3))
    ).reshape(block_count, rank_portion, BLOCK)
    up_terms = adapter_scale * jnp.einsum(
        "bwl,blk->bwk",
        rank_mine,
        cot_full.reshape(block_count, BLOCK, key_width),
        preferred_element_type=jnp.float32,
    )
    up_send = jnp.take(up_terms.astype(jnp.bfloat16), my_block, axis=0)
    up_send = up_send * my_valid[:, None, None].astype(jnp.bfloat16)
    got_up_terms = exchange(up_send)

    grad_tokens = token_grads(
        cot_full, frozen_key_weight, rank_grad, live_rows, got_down, my_slot, own_blocks
    )
    grad_down = owner_sum(got_terms, in_adapter, in_valid, adapters, min(width, 512))
    grad_up = owner_sum(got_up_terms, in_adapter, in_valid, adapters, key_width)
    return (projected, grad_tokens, jnp.transpose(grad_down, (0, 2, 1)), grad_up)


def solution(mesh):
    placed = (
        P(("groups", "job"), "tensor"),
        P("tensor", None),
        P("job", "tensor", None),
        P("job", "tensor", None),
        P(("groups", "job", "tensor"), None),
        P("groups", None),
        P("groups"),
        P("groups"),
    )
    return jax.shard_map(
        local,
        mesh=mesh,
        in_specs=placed,
        out_specs=(
            P(("groups", "job", "tensor"), None),
            P(("groups", "job"), "tensor"),
            P(("groups", "job"), "tensor", None),
            P(("groups", "job"), "tensor", None),
        ),
        check_vma=False,
    )
```

```python
import functools

import jax
import jax.numpy as jnp
from jax import lax
from jax.experimental import pallas as pl
from jax.experimental.pallas import tpu as pltpu
from jax.sharding import PartitionSpec as P

BLOCK = 128
SLOT_CAP = 4
VMEM_LIMIT = 48 * 1024 * 1024


adapter_scale = 2.0

NT = (((1,), (1,)), ((), ()))
TN = (((0,), (0,)), ((), ()))


def dot(a, b, dims):
    return lax.dot_general(a, b, dims, preferred_element_type=jnp.float32)


def general(
    tokens,
    frozen_key_weight,
    adapter_down_maps,
    adapter_up_maps,
    cotangent,
    block_owner_job,
    block_local_adapter,
    block_live_rows,
):
    job_count = lax.axis_size("job")
    own_job = lax.axis_index("job")
    row_total = tokens.shape[0]
    block_count = row_total // BLOCK
    local_adapters = adapter_down_maps.shape[0]
    width_portion = adapter_down_maps.shape[1]
    full_rank_values = adapter_down_maps.shape[2]
    rank_portion = adapter_up_maps.shape[1]
    output_width = adapter_up_maps.shape[2]
    owners_all = block_owner_job[:, 0].reshape(job_count, block_count)
    locals_all = block_local_adapter.reshape(job_count, block_count)
    fills_all = block_live_rows.reshape(job_count, block_count)
    my_owner = lax.dynamic_index_in_dim(owners_all, own_job, 0, keepdims=False)
    my_local = lax.dynamic_index_in_dim(locals_all, own_job, 0, keepdims=False)
    my_fill = lax.dynamic_index_in_dim(fills_all, own_job, 0, keepdims=False)
    adapter_ids = my_owner * local_adapters + my_local
    live_rows = (jnp.arange(BLOCK, dtype=jnp.int32)[None, :] < my_fill[:, None]).reshape(row_total)
    masked = tokens * live_rows[:, None].astype(jnp.bfloat16)
    row_blocks = masked.reshape(block_count, BLOCK, width_portion)
    every_down, every_up = (
        lax.all_gather(adapter_down_maps, "job", axis=0, tiled=True),
        lax.all_gather(adapter_up_maps, "job", axis=0, tiled=True),
    )
    block_down_maps = jnp.take(every_down, adapter_ids, axis=0)
    up_blocks = jnp.take(every_up, adapter_ids, axis=0)
    rank_terms = jnp.einsum(
        "bnd,bdr->bnr", row_blocks, block_down_maps, preferred_element_type=jnp.float32
    ).reshape(row_total, full_rank_values)
    rank_mine = lax.psum_scatter(
        rank_terms.astype(jnp.bfloat16), "tensor", scatter_dimension=1, tiled=True
    ).astype(jnp.float32)
    rank_blocks = rank_mine.reshape(block_count, BLOCK, rank_portion)
    adapter_rows = jnp.einsum(
        "seu,sui->sei", rank_blocks, up_blocks.astype(jnp.float32), precision=lax.Precision.HIGHEST
    ).reshape(row_total, output_width)
    projected = lax.psum_scatter(
        (
            jnp.dot(masked, frozen_key_weight, preferred_element_type=jnp.float32)
            + adapter_scale * adapter_rows
        ).astype(jnp.bfloat16),
        "tensor",
        scatter_dimension=0,
        tiled=True,
    )
    grad_full = lax.all_gather(cotangent, "tensor", axis=0, tiled=True)
    grad_blocks = grad_full.reshape(block_count, BLOCK, output_width)
    rank_grad_mine = (
        adapter_scale
        * jnp.einsum("ald,afd->alf", grad_blocks, up_blocks, preferred_element_type=jnp.float32)
    ).astype(jnp.bfloat16)
    rank_grad_all = lax.all_gather(
        rank_grad_mine.reshape(row_total, rank_portion), "tensor", axis=1, tiled=True
    )
    rank_grad_blocks = rank_grad_all.reshape(block_count, BLOCK, full_rank_values)
    grad_rows = lax.dot_general(
        grad_full, frozen_key_weight, (((1,), (1,)), ((), ())), preferred_element_type=jnp.float32
    )
    grad_rows = grad_rows + jnp.einsum(
        "bnr,bdr->bnd", rank_grad_blocks, block_down_maps, preferred_element_type=jnp.float32
    ).reshape(row_total, width_portion)
    grad_tokens = (grad_rows * live_rows[:, None].astype(jnp.float32)).astype(jnp.bfloat16)
    down_terms = jnp.einsum(
        "bnd,bnr->bdr", row_blocks, rank_grad_blocks, preferred_element_type=jnp.float32
    ).reshape(block_count, -1)
    up_map_terms = (
        adapter_scale
        * jnp.einsum(
            "xhw,xhk->xwk",
            rank_blocks,
            grad_blocks.astype(jnp.float32),
            precision=lax.Precision.HIGHEST,
        )
    ).reshape(block_count, -1)
    adapter_range = jnp.arange(job_count * local_adapters, dtype=jnp.int32)
    onehot = (adapter_ids[None, :] == adapter_range[:, None]).astype(jnp.float32)
    dense_down = jnp.einsum(
        "ab,bx->ax", onehot, down_terms, precision=lax.Precision.HIGHEST
    ).reshape(job_count, local_adapters, -1)
    dense_up = jnp.einsum(
        "ab,bx->ax", onehot, up_map_terms, precision=lax.Precision.HIGHEST
    ).reshape(job_count, local_adapters, -1)
    got_down, got_up = (
        lax.all_to_all(
            dense_down.astype(jnp.bfloat16), "job", split_axis=0, concat_axis=0, tiled=True
        ).astype(dense_down.dtype),
        lax.all_to_all(
            dense_up.astype(jnp.bfloat16), "job", split_axis=0, concat_axis=0, tiled=True
        ).astype(dense_up.dtype),
    )
    grad_down = jnp.sum(got_down, axis=0)
    grad_up = jnp.sum(got_up, axis=0)
    grad_down = grad_down.reshape(local_adapters, width_portion, full_rank_values)
    grad_up = grad_up.reshape(local_adapters, rank_portion, output_width)
    return (projected, grad_tokens, grad_down, grad_up)


def peers_of(own, groups):
    x, core = own // 2, own % 2
    return (2 * (1 - x) + core, 2 * (1 - x) + 1 - core, 2 * x + 1 - core)


def main_kernel(
    n,
    owner_ref,
    local_ref,
    fill_ref,
    tokens_in,
    weight_in,
    down_in,
    up_in,
    cot_in,
    projected_ref,
    grad_tokens_out,
    got_terms,
    got_up_terms,
    tokens,
    weight,
    down_all,
    up_all,
    cot,
    part,
    from_left,
    from_right,
    up_turn,
    up_own,
    rank_grad,
    rank_part,
    rank_in,
    rank_split,
    rank_mine,
    term_send,
    up_term_send,
    staged,
    load_sem,
    send_sem,
    recv_sem,
):
    group = lax.axis_index("groups")
    job = lax.axis_index("job")
    me = lax.axis_index("tensor")
    blocks = tokens.shape[0]
    own_blocks = blocks // n
    width = tokens.shape[2]
    key_width = weight.shape[1]
    adapters = down_in.shape[0]
    rank = down_in.shape[1]
    portion = rank // n
    jobs = 4
    half = adapters // 2
    jx, jd, js = peers_of(job, None)
    counter = [0]
    loads = [0]

    def remote(src, dst, where):
        k = counter[0]
        counter[0] += 1
        return pltpu.make_async_remote_copy(
            src_ref=src,
            dst_ref=dst,
            send_sem=send_sem.at[k],
            recv_sem=recv_sem.at[k],
            device_id=where,
            device_id_type=pl.DeviceIdType.MESH,
        )

    def load(src, dst):
        k = loads[0]
        loads[0] += 1
        copy = pltpu.make_async_copy(src, dst, load_sem.at[k])
        copy.start()
        return copy

    others = [lax.rem(me + r, n) for r in range(1, n)]

    own_slice = pl.ds(me * own_blocks, own_blocks)
    cot_load = load(cot_in, cot.at[own_slice])
    weight_load = load(weight_in, weight)
    tokens_load = load(tokens_in, tokens)
    up_load = load(up_in, up_all.at[pl.ds(job * adapters, adapters)])
    down_load = load(down_in, down_all.at[pl.ds(job * adapters, adapters)])

    barrier = pltpu.get_barrier_semaphore()
    for p in (jx, jd, js):
        pl.semaphore_signal(
            barrier, inc=1, device_id={"job": p}, device_id_type=pl.DeviceIdType.MESH
        )
    for p in others:
        pl.semaphore_signal(
            barrier, inc=1, device_id={"tensor": p}, device_id_type=pl.DeviceIdType.MESH
        )
    pl.semaphore_signal(
        barrier, inc=1, device_id={"groups": 1 - group}, device_id_type=pl.DeviceIdType.MESH
    )
    pl.semaphore_wait(barrier, 3 + len(others) + 1)

    up_copies = [
        remote(up_in, up_all.at[pl.ds(job * adapters, adapters)], {"job": p}) for p in (jx, jd, js)
    ]
    for c in up_copies:
        c.start()

    def chunk(index):
        return pl.ds(index * own_blocks, own_blocks)

    right_gather, left_gather = [], []
    for s in range(n - 1):
        rs, ls = jnp.clip(me - s, 0, n - 1), jnp.clip(me + s, 0, n - 1)
        right_gather.append(
            remote(
                cot_in if s == 0 else cot.at[chunk(rs)],
                cot.at[chunk(rs)],
                {"tensor": jnp.minimum(me + 1, n - 1)},
            )
        )
        left_gather.append(
            remote(
                cot_in if s == 0 else cot.at[chunk(ls)],
                cot.at[chunk(ls)],
                {"tensor": jnp.maximum(me - 1, 0)},
            )
        )

    def gather_send(s):
        @pl.when((me >= s) & (me <= n - 2))
        def _():
            right_gather[s].start()

        @pl.when((me <= n - 1 - s) & (me >= 1))
        def _():
            left_gather[s].start()

    def gather_recv(s):
        @pl.when(me - 1 >= s)
        def _():
            right_gather[s].wait_recv()

        @pl.when(me + 1 <= n - 1 - s)
        def _():
            left_gather[s].wait_recv()

    gather_send(0)

    def region(owner, h):
        return down_all.at[pl.ds(owner * adapters + h * half, half)]

    copy_a = remote(down_in.at[pl.ds(group * half, half)], region(job, group), {"job": jx})
    copy_b = remote(down_in, down_all.at[pl.ds(job * adapters, adapters)], {"job": js})
    copy_c = remote(region(jx, group), region(jx, group), {"groups": 1 - group})
    copy_d = remote(region(jx, group), region(jx, group), {"job": js})
    copy_e = remote(region(jx, 1 - group), region(jx, 1 - group), {"job": js})
    copy_a.start()
    copy_b.start()

    base = job * blocks
    owner = [owner_ref[base + b] for b in range(blocks)]
    adapter = [owner[b] * adapters + local_ref[base + b] for b in range(blocks)]
    fill = [fill_ref[base + b] for b in range(blocks)]
    place = []
    for b in range(blocks):
        total = jnp.int32(0)
        for e in range(b):
            total = total + jnp.where(owner[e] == owner[b], 1, 0)
        place.append(total)

    def slot(o, s):
        index, valid = jnp.int32(0), jnp.int32(0)
        for b in range(blocks):
            hit = jnp.where((owner[b] == o) & (place[b] == s), 1, 0)
            index, valid = index + b * hit, valid + hit
        return index, valid

    def live_column(b):
        return lax.broadcasted_iota(jnp.int32, (BLOCK, 1), 0) < fill[b]

    def live_row(b):
        return lax.broadcasted_iota(jnp.int32, (1, BLOCK), 1) < fill[b]

    weight_load.wait()
    tokens_load.wait()
    tile = 256
    per = blocks // 2
    for h in range(2):
        masks = [live_column(h * per + k) for k in range(per)]

        @pl.loop(0, key_width // tile)
        def _(t, h=h, masks=masks):
            columns = pl.ds(pl.multiple_of(t * tile, tile), tile)
            rows = tokens[pl.ds(h * per, per)].reshape(per * BLOCK, width)
            acc = jnp.dot(rows, weight[:, columns], preferred_element_type=jnp.float32)
            for k in range(per):
                part[h * per + k, :, columns] = jnp.where(
                    masks[k], acc[k * BLOCK : (k + 1) * BLOCK], 0.0
                ).astype(part.dtype)

    up_load.wait()
    for c in up_copies:
        c.wait_recv()
    turn_copies = [
        remote(up_turn.at[p], up_own.at[me], {"tensor": p}) for p in others
    ]
    for b in range(blocks):
        up_turn[b // own_blocks, b % own_blocks] = up_all[adapter[b]]
    for c in turn_copies:
        c.start()
    up_own[me] = up_turn[me]

    cot_load.wait()
    gather_recv(0)
    gather_send(1)

    right_sum, left_sum = [], []
    for s in range(n - 1):
        rd = jnp.clip(n - 1 - s + me, 0, n - 1)
        ld = jnp.clip(s - (n - 1 - me), 0, n - 1)
        right_sum.append(
            (
                rd,
                remote(
                    part.at[chunk(rd)], from_left.at[s], {"tensor": jnp.minimum(me + 1, n - 1)}
                ),
            )
        )
        left_sum.append(
            (
                ld,
                remote(part.at[chunk(ld)], from_right.at[s], {"tensor": jnp.maximum(me - 1, 0)}),
            )
        )

    def add_into(index, got):
        for k in range(own_blocks):
            b = index * own_blocks + k
            part[b] = (part[b].astype(jnp.float32) + got[k].astype(jnp.float32)).astype(part.dtype)

    def sum_send(s):
        mirrored = n - 1 - me

        @pl.when((me <= s) & (me <= n - 2))
        def _():
            index, copy = right_sum[s]
            if s > 0:

                @pl.when(me >= 1)
                def _():
                    right_sum[s - 1][1].wait_recv()
                    add_into(index, from_left.at[s - 1])

            copy.start()

        @pl.when((mirrored <= s) & (mirrored <= n - 2))
        def _():
            index, copy = left_sum[s]
            if s > 0:

                @pl.when(mirrored >= 1)
                def _():
                    left_sum[s - 1][1].wait_recv()
                    add_into(index, from_right.at[s - 1])

            copy.start()

    sum_send(0)

    for c in turn_copies:
        c.wait_recv()
    up_full = [up_own[:, k].reshape(rank, key_width) for k in range(own_blocks)]
    for k in range(own_blocks):
        value = dot(up_full[k], cot[me * own_blocks + k], NT)
        rank_grad[me * own_blocks + k] = (adapter_scale * value).astype(rank_grad.dtype)
    grad_copies = [
        remote(rank_grad.at[chunk(me)], rank_grad.at[chunk(me)], {"tensor": p}) for p in others
    ]
    for c in grad_copies:
        c.start()

    copy_a.wait_recv()
    copy_c.start()
    copy_d.start()
    for c in grad_copies:
        c.wait_recv()

    term_copies = []
    for i, p in enumerate((jx, jd, js, job)):
        for s in range(SLOT_CAP):
            index, valid = slot(p, s)
            live = lax.broadcasted_iota(jnp.int32, (1, BLOCK), 1) < (
                fill_ref[base + index] * valid
            )
            rows = jnp.where(live, rank_grad[index].astype(jnp.float32), 0.0).astype(
                rank_grad.dtype
            )
            term_send[i, s] = jnp.dot(
                rows, tokens[index], preferred_element_type=jnp.float32
            ).astype(term_send.dtype)
        if i < 3:
            c = remote(term_send.at[i], got_terms.at[job], {"job": p})
            c.start()
            term_copies.append(c)
        else:
            own_terms = load(term_send.at[i], got_terms.at[job])
        if i == 1:
            gather_recv(1)
            if n > 3:
                gather_send(2)
            sum_send(1)

    copy_c.wait_recv()
    copy_e.start()
    for s in range(2, n - 1):
        gather_recv(s)
        if s + 1 < n - 1:
            gather_send(s + 1)
        sum_send(s)
    down_load.wait()
    copy_b.wait_recv()
    copy_d.wait_recv()
    copy_e.wait_recv()

    for b in range(blocks):
        value = dot(down_all[adapter[b]], tokens[b], NT)
        rank_part[b // own_blocks, b % own_blocks] = jnp.where(live_row(b), value, 0.0).astype(
            rank_part.dtype
        )
    rank_copies = [remote(rank_part.at[p], rank_in.at[me], {"tensor": p}) for p in others]
    for c in rank_copies:
        c.start()

    out_copies = []
    tile_out = 512

    def token_chunk(z):
        @pl.loop(0, width // tile_out)
        def _(t):
            columns = pl.ds(pl.multiple_of(t * tile_out, tile_out), tile_out)
            rows = cot[pl.ds(z * own_blocks, own_blocks)].reshape(own_blocks * BLOCK, key_width)
            acc = dot(rows, weight[columns, :], NT)
            for k in range(own_blocks):
                b = z * own_blocks + k
                value = acc[k * BLOCK : (k + 1) * BLOCK] + dot(
                    rank_grad[b], down_all[adapter[b], :, columns], TN
                )
                staged[b, :, columns] = jnp.where(live_column(b), value, 0.0).astype(staged.dtype)

        out_copies.append(
            load(
                staged.at[pl.ds(z * own_blocks, own_blocks)],
                grad_tokens_out.at[pl.ds(z * own_blocks, own_blocks)],
            )
        )

    for z in range(n // 2):
        token_chunk(z)

    for c in rank_copies:
        c.wait_recv()
    rank_in[me] = rank_part[me]
    rank_sum = jnp.sum(rank_in[...].astype(jnp.float32), axis=0)
    rank_sum = rank_sum.astype(jnp.bfloat16)
    for t in range(n):
        rank_split[t] = rank_sum[:, t * portion : (t + 1) * portion]
    mine_copies = [remote(rank_split.at[p], rank_mine.at[chunk(me)], {"tensor": p}) for p in others]
    for c in mine_copies:
        c.start()
    for k in range(own_blocks):
        rank_mine[me * own_blocks + k] = rank_split[me, k]

    for z in range(n // 2, n):
        token_chunk(z)

    for c in mine_copies:
        c.wait_recv()
    up_term_copies = []
    for i, p in enumerate((jx, jd, js, job)):
        for s in range(SLOT_CAP):
            index, valid = slot(p, s)
            value = jnp.dot(rank_mine[index], cot[index], preferred_element_type=jnp.float32)
            up_term_send[i, s] = (
                jnp.where(valid > 0, adapter_scale, 0.0) * value
            ).astype(up_term_send.dtype)
        if i < 3:
            c = remote(up_term_send.at[i], got_up_terms.at[job], {"job": p})
            c.start()
            up_term_copies.append(c)
        else:
            own_up_terms = load(up_term_send.at[i], got_up_terms.at[job])

    @pl.when(me >= 1)
    def _():
        right_sum[n - 2][1].wait_recv()

    @pl.when(me <= n - 2)
    def _():
        left_sum[n - 2][1].wait_recv()

    for k in range(own_blocks):
        value = part[me * own_blocks + k].astype(jnp.float32) + adapter_scale * dot(
            rank_sum[k], up_own[:, k].reshape(rank, key_width), TN
        )
        value = value + jnp.where(me >= 1, from_left[n - 2, k].astype(jnp.float32), 0.0)
        value = value + jnp.where(me <= n - 2, from_right[n - 2, k].astype(jnp.float32), 0.0)
        projected_ref[pl.ds(k * BLOCK, BLOCK), :] = value.astype(projected_ref.dtype)

    for c in term_copies + up_term_copies:
        c.wait_recv()
    for c in (
        up_copies
        + [copy_a, copy_b, copy_c, copy_d, copy_e]
        + turn_copies
        + grad_copies
        + term_copies
        + rank_copies
        + mine_copies
        + up_term_copies
    ):
        c.wait_send()
    for s in range(n - 1):

        @pl.when((me >= s) & (me <= n - 2))
        def _(s=s):
            right_gather[s].wait_send()

        @pl.when((me <= n - 1 - s) & (me >= 1))
        def _(s=s):
            left_gather[s].wait_send()

        @pl.when((me <= s) & (me <= n - 2))
        def _(s=s):
            right_sum[s][1].wait_send()

        @pl.when((n - 1 - me <= s) & (me >= 1))
        def _(s=s):
            left_sum[s][1].wait_send()

    own_terms.wait()
    own_up_terms.wait()
    for c in out_copies:
        c.wait()


def owner_sum_kernel(blocks, own_ref, owner_ref, local_ref, got_ref, got_up_ref, down_ref, up_ref):
    own = own_ref[0]
    first = pl.program_id(0) == 0
    down_ref[...] = jnp.zeros_like(down_ref)

    @pl.when(first)
    def _():
        up_ref[...] = jnp.zeros_like(up_ref)

    for j in range(got_ref.shape[0]):
        def step(b, count, j=j):
            hit = owner_ref[j * blocks + b] == own
            a = local_ref[j * blocks + b]

            @pl.when(hit)
            def _():
                down_ref[a] = down_ref[a] + got_ref[j, count].astype(jnp.float32)

            @pl.when(hit & first)
            def _():
                up_ref[a] = up_ref[a] + got_up_ref[j, count].astype(jnp.float32)

            return count + jnp.where(hit, 1, 0)

        lax.fori_loop(0, blocks, step, jnp.int32(0))


def owner_sum(own, owners, locals_all, got, got_up, adapters, blocks, tile):
    jobs, slots, rank, width = got.shape
    portion, key_width = got_up.shape[2:]
    return pl.pallas_call(
        functools.partial(owner_sum_kernel, blocks),
        grid_spec=pltpu.PrefetchScalarGridSpec(
            num_scalar_prefetch=3,
            grid=(width // tile,),
            in_specs=[
                pl.BlockSpec((jobs, slots, rank, tile), lambda i, *_: (0, 0, 0, i)),
                pl.BlockSpec((jobs, slots, portion, key_width), lambda i, *_: (0, 0, 0, 0)),
            ],
            out_specs=[
                pl.BlockSpec((adapters, rank, tile), lambda i, *_: (0, 0, i)),
                pl.BlockSpec((adapters, portion, key_width), lambda i, *_: (0, 0, 0)),
            ],
        ),
        out_shape=[
            jax.ShapeDtypeStruct((adapters, rank, width), jnp.float32),
            jax.ShapeDtypeStruct((adapters, portion, key_width), jnp.float32),
        ],
        compiler_params=pltpu.CompilerParams(vmem_limit_bytes=VMEM_LIMIT),
        name="owner_sum",
    )(own, owners, locals_all, got, got_up)


def local(
    tokens,
    frozen_key_weight,
    adapter_down_maps,
    adapter_up_maps,
    cotangent,
    block_owner_job,
    block_local_adapter,
    block_live_rows,
):
    own_rows, key_width = cotangent.shape
    n = lax.axis_size("tensor")
    jobs = lax.axis_size("job")
    adapters, width, rank = adapter_down_maps.shape
    portion = adapter_up_maps.shape[1]
    fits = own_rows % BLOCK == 0 and n >= 3 and n % 2 == 0 and jobs == 4
    if not (fits and lax.axis_size("groups") == 2 and adapters % 2 == 0 and portion == 16):
        return general(
            tokens,
            frozen_key_weight,
            adapter_down_maps,
            adapter_up_maps,
            cotangent,
            block_owner_job,
            block_local_adapter,
            block_live_rows,
        )
    row_total = tokens.shape[0]
    blocks = row_total // BLOCK
    own_blocks = own_rows // BLOCK
    owners = block_owner_job.reshape(-1)
    bf16 = jnp.bfloat16
    hbm = pl.BlockSpec(memory_space=pl.ANY)
    smem = pl.BlockSpec(memory_space=pltpu.SMEM)
    copies = 3 + 4 * (n - 1) + 5 + 4 * (n - 1) + 6
    projected, grad_tokens, got_terms, got_up_terms = pl.pallas_call(
        functools.partial(main_kernel, n),
        in_specs=[smem, smem, smem, hbm, hbm, hbm, hbm, hbm],
        out_specs=[pl.BlockSpec(memory_space=pltpu.VMEM), hbm, hbm, hbm],
        out_shape=[
            jax.ShapeDtypeStruct((own_rows, key_width), bf16),
            jax.ShapeDtypeStruct((blocks, BLOCK, width), bf16),
            jax.ShapeDtypeStruct((jobs, SLOT_CAP, rank, width), bf16),
            jax.ShapeDtypeStruct((jobs, SLOT_CAP, portion, key_width), bf16),
        ],
        scratch_shapes=[
            pltpu.VMEM((blocks, BLOCK, width), bf16),
            pltpu.VMEM(frozen_key_weight.shape, bf16),
            pltpu.VMEM((jobs * adapters, rank, width), bf16),
            pltpu.VMEM((jobs * adapters, portion, key_width), bf16),
            pltpu.VMEM((blocks, BLOCK, key_width), bf16),
            pltpu.VMEM((blocks, BLOCK, key_width), bf16),
            pltpu.VMEM((n - 1, own_blocks, BLOCK, key_width), bf16),
            pltpu.VMEM((n - 1, own_blocks, BLOCK, key_width), bf16),
            pltpu.VMEM((n, own_blocks, portion, key_width), bf16),
            pltpu.VMEM((n, own_blocks, portion, key_width), bf16),
            pltpu.VMEM((blocks, rank, BLOCK), bf16),
            pltpu.VMEM((n, own_blocks, rank, BLOCK), bf16),
            pltpu.VMEM((n, own_blocks, rank, BLOCK), bf16),
            pltpu.VMEM((n, own_blocks, portion, BLOCK), bf16),
            pltpu.VMEM((blocks, portion, BLOCK), bf16),
            pltpu.VMEM((jobs, SLOT_CAP, rank, width), bf16),
            pltpu.VMEM((jobs, SLOT_CAP, portion, key_width), bf16),
            pltpu.VMEM((blocks, BLOCK, width), bf16),
            pltpu.SemaphoreType.DMA((7 + n,)),
            pltpu.SemaphoreType.DMA((copies,)),
            pltpu.SemaphoreType.DMA((copies,)),
        ],
        compiler_params=pltpu.CompilerParams(
            collective_id=0, has_side_effects=True, vmem_limit_bytes=60 * 1024 * 1024
        ),
        cost_estimate=pl.CostEstimate(
            flops=4 * row_total * width * key_width,
            bytes_accessed=4 * row_total * width,
            transcendentals=0,
        ),
        name="project_and_grads",
    )(
        owners,
        block_local_adapter,
        block_live_rows,
        tokens.reshape(blocks, BLOCK, width),
        frozen_key_weight,
        jnp.transpose(adapter_down_maps, (0, 2, 1)),
        adapter_up_maps,
        cotangent.reshape(own_blocks, BLOCK, key_width),
    )
    own = lax.axis_index("job").astype(jnp.int32).reshape(1)
    grad_down, grad_up = owner_sum(
        own, owners, block_local_adapter, got_terms, got_up_terms, adapters, blocks, 512
    )
    return (
        projected,
        grad_tokens.reshape(row_total, width),
        jnp.transpose(grad_down, (0, 2, 1)),
        grad_up,
    )


def solution(mesh):
    placed = (
        P(("groups", "job"), "tensor"),
        P("tensor", None),
        P("job", "tensor", None),
        P("job", "tensor", None),
        P(("groups", "job", "tensor"), None),
        P("groups", None),
        P("groups"),
        P("groups"),
    )
    return jax.shard_map(
        local,
        mesh=mesh,
        in_specs=placed,
        out_specs=(
            P(("groups", "job", "tensor"), None),
            P(("groups", "job"), "tensor"),
            P(("groups", "job"), "tensor", None),
            P(("groups", "job"), "tensor", None),
        ),
        check_vma=False,
    )
```

```python
import functools

import jax
import jax.numpy as jnp
from jax import lax
from jax.experimental import pallas as pl
from jax.experimental.pallas import tpu as pltpu
from jax.sharding import PartitionSpec as P

BLOCK = 128
SLOT_CAP = 4
VMEM_LIMIT = 48 * 1024 * 1024


adapter_scale = 2.0

NT = (((1,), (1,)), ((), ()))
TN = (((0,), (0,)), ((), ()))


def dot(a, b, dims):
    return lax.dot_general(a, b, dims, preferred_element_type=jnp.float32)


def general(
    tokens,
    frozen_key_weight,
    adapter_down_maps,
    adapter_up_maps,
    cotangent,
    block_owner_job,
    block_local_adapter,
    block_live_rows,
):
    job_count = lax.axis_size("job")
    own_job = lax.axis_index("job")
    row_total = tokens.shape[0]
    block_count = row_total // BLOCK
    local_adapters = adapter_down_maps.shape[0]
    width_portion = adapter_down_maps.shape[1]
    full_rank_values = adapter_down_maps.shape[2]
    rank_portion = adapter_up_maps.shape[1]
    output_width = adapter_up_maps.shape[2]
    owners_all = block_owner_job[:, 0].reshape(job_count, block_count)
    locals_all = block_local_adapter.reshape(job_count, block_count)
    fills_all = block_live_rows.reshape(job_count, block_count)
    my_owner = lax.dynamic_index_in_dim(owners_all, own_job, 0, keepdims=False)
    my_local = lax.dynamic_index_in_dim(locals_all, own_job, 0, keepdims=False)
    my_fill = lax.dynamic_index_in_dim(fills_all, own_job, 0, keepdims=False)
    adapter_ids = my_owner * local_adapters + my_local
    live_rows = (jnp.arange(BLOCK, dtype=jnp.int32)[None, :] < my_fill[:, None]).reshape(row_total)
    masked = tokens * live_rows[:, None].astype(jnp.bfloat16)
    row_blocks = masked.reshape(block_count, BLOCK, width_portion)
    every_down, every_up = (
        lax.all_gather(adapter_down_maps, "job", axis=0, tiled=True),
        lax.all_gather(adapter_up_maps, "job", axis=0, tiled=True),
    )
    block_down_maps = jnp.take(every_down, adapter_ids, axis=0)
    up_blocks = jnp.take(every_up, adapter_ids, axis=0)
    rank_terms = jnp.einsum(
        "bnd,bdr->bnr", row_blocks, block_down_maps, preferred_element_type=jnp.float32
    ).reshape(row_total, full_rank_values)
    rank_mine = lax.psum_scatter(
        rank_terms.astype(jnp.bfloat16), "tensor", scatter_dimension=1, tiled=True
    ).astype(jnp.float32)
    rank_blocks = rank_mine.reshape(block_count, BLOCK, rank_portion)
    adapter_rows = jnp.einsum(
        "seu,sui->sei", rank_blocks, up_blocks.astype(jnp.float32), precision=lax.Precision.HIGHEST
    ).reshape(row_total, output_width)
    projected = lax.psum_scatter(
        (
            jnp.dot(masked, frozen_key_weight, preferred_element_type=jnp.float32)
            + adapter_scale * adapter_rows
        ).astype(jnp.bfloat16),
        "tensor",
        scatter_dimension=0,
        tiled=True,
    )
    grad_full = lax.all_gather(cotangent, "tensor", axis=0, tiled=True)
    grad_blocks = grad_full.reshape(block_count, BLOCK, output_width)
    rank_grad_mine = (
        adapter_scale
        * jnp.einsum("ald,afd->alf", grad_blocks, up_blocks, preferred_element_type=jnp.float32)
    ).astype(jnp.bfloat16)
    rank_grad_all = lax.all_gather(
        rank_grad_mine.reshape(row_total, rank_portion), "tensor", axis=1, tiled=True
    )
    rank_grad_blocks = rank_grad_all.reshape(block_count, BLOCK, full_rank_values)
    grad_rows = lax.dot_general(
        grad_full, frozen_key_weight, (((1,), (1,)), ((), ())), preferred_element_type=jnp.float32
    )
    grad_rows = grad_rows + jnp.einsum(
        "bnr,bdr->bnd", rank_grad_blocks, block_down_maps, preferred_element_type=jnp.float32
    ).reshape(row_total, width_portion)
    grad_tokens = (grad_rows * live_rows[:, None].astype(jnp.float32)).astype(jnp.bfloat16)
    down_terms = jnp.einsum(
        "bnd,bnr->bdr", row_blocks, rank_grad_blocks, preferred_element_type=jnp.float32
    ).reshape(block_count, -1)
    up_map_terms = (
        adapter_scale
        * jnp.einsum(
            "xhw,xhk->xwk",
            rank_blocks,
            grad_blocks.astype(jnp.float32),
            precision=lax.Precision.HIGHEST,
        )
    ).reshape(block_count, -1)
    adapter_range = jnp.arange(job_count * local_adapters, dtype=jnp.int32)
    onehot = (adapter_ids[None, :] == adapter_range[:, None]).astype(jnp.float32)
    dense_down = jnp.einsum(
        "ab,bx->ax", onehot, down_terms, precision=lax.Precision.HIGHEST
    ).reshape(job_count, local_adapters, -1)
    dense_up = jnp.einsum(
        "ab,bx->ax", onehot, up_map_terms, precision=lax.Precision.HIGHEST
    ).reshape(job_count, local_adapters, -1)
    got_down, got_up = (
        lax.all_to_all(
            dense_down.astype(jnp.bfloat16), "job", split_axis=0, concat_axis=0, tiled=True
        ).astype(dense_down.dtype),
        lax.all_to_all(
            dense_up.astype(jnp.bfloat16), "job", split_axis=0, concat_axis=0, tiled=True
        ).astype(dense_up.dtype),
    )
    grad_down = jnp.sum(got_down, axis=0)
    grad_up = jnp.sum(got_up, axis=0)
    grad_down = grad_down.reshape(local_adapters, width_portion, full_rank_values)
    grad_up = grad_up.reshape(local_adapters, rank_portion, output_width)
    return (projected, grad_tokens, grad_down, grad_up)


def peers_of(own):
    x, core = own // 2, own % 2
    return (2 * (1 - x) + core, 2 * (1 - x) + 1 - core, 2 * x + 1 - core)


def main_kernel(
    n,
    owner_ref,
    local_ref,
    fill_ref,
    tokens_in,
    weight_in,
    down_in,
    up_in,
    cot_in,
    projected_ref,
    grad_tokens_out,
    grad_down_out,
    grad_up_out,
    tokens,
    weight,
    down_all,
    up_all,
    cot,
    part,
    from_left,
    from_right,
    up_turn,
    up_own,
    rank_grad,
    rank_part,
    rank_in,
    rank_split,
    rank_mine,
    term_send,
    up_term_send,
    staged,
    got_terms,
    got_up_terms,
    down_total,
    load_sem,
    send_sem,
    recv_sem,
):
    group = lax.axis_index("groups")
    job = lax.axis_index("job")
    me = lax.axis_index("tensor")
    blocks = tokens.shape[0]
    own_blocks = blocks // n
    width = tokens.shape[2]
    key_width = weight.shape[1]
    adapters = down_in.shape[0]
    rank = down_in.shape[1]
    portion = rank // n
    jobs = 4
    half = adapters // 2
    jx, jd, js = peers_of(job)
    counter = [0]
    loads = [0]

    def remote(src, dst, where):
        k = counter[0]
        counter[0] += 1
        return pltpu.make_async_remote_copy(
            src_ref=src,
            dst_ref=dst,
            send_sem=send_sem.at[k],
            recv_sem=recv_sem.at[k],
            device_id=where,
            device_id_type=pl.DeviceIdType.MESH,
        )

    def load(src, dst):
        k = loads[0]
        loads[0] += 1
        copy = pltpu.make_async_copy(src, dst, load_sem.at[k])
        copy.start()
        return copy

    others = [lax.rem(me + r, n) for r in range(1, n)]

    own_slice = pl.ds(me * own_blocks, own_blocks)
    cot_load = load(cot_in, cot.at[own_slice])
    weight_load = load(weight_in, weight)
    tokens_load = load(tokens_in, tokens)
    up_load = load(up_in, up_all.at[pl.ds(job * adapters, adapters)])
    down_load = load(down_in, down_all.at[pl.ds(job * adapters, adapters)])

    barrier = pltpu.get_barrier_semaphore()
    for p in (jx, jd, js):
        pl.semaphore_signal(
            barrier, inc=1, device_id={"job": p}, device_id_type=pl.DeviceIdType.MESH
        )
    for p in others:
        pl.semaphore_signal(
            barrier, inc=1, device_id={"tensor": p}, device_id_type=pl.DeviceIdType.MESH
        )
    pl.semaphore_signal(
        barrier, inc=1, device_id={"groups": 1 - group}, device_id_type=pl.DeviceIdType.MESH
    )
    pl.semaphore_wait(barrier, 3 + len(others) + 1)

    up_copies = [
        remote(up_in, up_all.at[pl.ds(job * adapters, adapters)], {"job": p}) for p in (jx, js)
    ]
    for c in up_copies:
        c.start()
    jx_maps = up_all.at[pl.ds(jx * adapters, adapters)]
    up_copies.append(remote(jx_maps, jx_maps, {"job": js}))

    def chunk(index):
        return pl.ds(index * own_blocks, own_blocks)

    right_gather, left_gather = [], []
    for s in range(n - 1):
        rs, ls = jnp.clip(me - s, 0, n - 1), jnp.clip(me + s, 0, n - 1)
        right_gather.append(
            remote(
                cot_in if s == 0 else cot.at[chunk(rs)],
                cot.at[chunk(rs)],
                {"tensor": jnp.minimum(me + 1, n - 1)},
            )
        )
        left_gather.append(
            remote(
                cot_in if s == 0 else cot.at[chunk(ls)],
                cot.at[chunk(ls)],
                {"tensor": jnp.maximum(me - 1, 0)},
            )
        )

    def gather_send(s):
        @pl.when((me >= s) & (me <= n - 2))
        def _():
            right_gather[s].start()

        @pl.when((me <= n - 1 - s) & (me >= 1))
        def _():
            left_gather[s].start()

    def gather_recv(s):
        @pl.when(me - 1 >= s)
        def _():
            right_gather[s].wait_recv()

        @pl.when(me + 1 <= n - 1 - s)
        def _():
            left_gather[s].wait_recv()

    gather_send(0)

    piece = half // 2

    def region(owner, h, i):
        return down_all.at[pl.ds(owner * adapters + h * half + i * piece, piece)]

    copy_a = [
        remote(
            down_in.at[pl.ds(group * half + i * piece, piece)], region(job, group, i), {"job": jx}
        )
        for i in range(2)
    ]
    copy_b = remote(down_in, down_all.at[pl.ds(job * adapters, adapters)], {"job": js})
    mine = [region(jx, group, i) for i in range(2)]
    other = [region(jx, 1 - group, i) for i in range(2)]
    copy_c = [remote(r, r, {"groups": 1 - group}) for r in mine]
    copy_d = [remote(r, r, {"job": js}) for r in mine]
    copy_e = [remote(r, r, {"job": js}) for r in other]
    copy_b.start()

    base = job * blocks
    owner = [owner_ref[base + b] for b in range(blocks)]
    adapter = [owner[b] * adapters + local_ref[base + b] for b in range(blocks)]
    fill = [fill_ref[base + b] for b in range(blocks)]
    place = []
    for b in range(blocks):
        total = jnp.int32(0)
        for e in range(b):
            total = total + jnp.where(owner[e] == owner[b], 1, 0)
        place.append(total)

    def slot(o, s):
        index, valid = jnp.int32(0), jnp.int32(0)
        for b in range(blocks):
            hit = jnp.where((owner[b] == o) & (place[b] == s), 1, 0)
            index, valid = index + b * hit, valid + hit
        return index, valid

    def live_column(b):
        return lax.broadcasted_iota(jnp.int32, (BLOCK, 1), 0) < fill[b]

    def live_row(b):
        return lax.broadcasted_iota(jnp.int32, (1, BLOCK), 1) < fill[b]

    weight_load.wait()
    tokens_load.wait()
    tile = 256
    per = blocks // 2

    def base_product(h):
        masks = [live_column(h * per + k) for k in range(per)]

        @pl.loop(0, key_width // tile)
        def _(t):
            columns = pl.ds(pl.multiple_of(t * tile, tile), tile)
            rows = tokens[pl.ds(h * per, per)].reshape(per * BLOCK, width)
            acc = jnp.dot(rows, weight[:, columns], preferred_element_type=jnp.float32)
            for k in range(per):
                part[h * per + k, :, columns] = jnp.where(
                    masks[k], acc[k * BLOCK : (k + 1) * BLOCK], 0.0
                ).astype(part.dtype)

    base_product(0)

    up_load.wait()
    up_copies[0].wait_recv()
    up_copies[2].start()
    for c in copy_a:
        c.start()
    up_copies[1].wait_recv()
    up_copies[2].wait_recv()
    turn_copies = [
        remote(up_turn.at[p], up_own.at[me], {"tensor": p}) for p in others
    ]
    for b in range(blocks):
        up_turn[b // own_blocks, b % own_blocks] = up_all[adapter[b]]
    for c in turn_copies:
        c.start()
    up_own[me] = up_turn[me]
    base_product(1)

    cot_load.wait()
    gather_recv(0)
    gather_send(1)

    right_sum, left_sum = [], []
    for s in range(n - 1):
        rd = jnp.clip(n - 1 - s + me, 0, n - 1)
        ld = jnp.clip(s - (n - 1 - me), 0, n - 1)
        right_sum.append(
            (
                rd,
                remote(
                    part.at[chunk(rd)], from_left.at[s], {"tensor": jnp.minimum(me + 1, n - 1)}
                ),
            )
        )
        left_sum.append(
            (
                ld,
                remote(part.at[chunk(ld)], from_right.at[s], {"tensor": jnp.maximum(me - 1, 0)}),
            )
        )

    def add_into(index, got):
        for k in range(own_blocks):
            b = index * own_blocks + k
            part[b] = (part[b].astype(jnp.float32) + got[k].astype(jnp.float32)).astype(part.dtype)

    def sum_send(s):
        mirrored = n - 1 - me

        @pl.when((me <= s) & (me <= n - 2))
        def _():
            index, copy = right_sum[s]
            if s > 0:

                @pl.when(me >= 1)
                def _():
                    right_sum[s - 1][1].wait_recv()
                    add_into(index, from_left.at[s - 1])

            copy.start()

        @pl.when((mirrored <= s) & (mirrored <= n - 2))
        def _():
            index, copy = left_sum[s]
            if s > 0:

                @pl.when(mirrored >= 1)
                def _():
                    left_sum[s - 1][1].wait_recv()
                    add_into(index, from_right.at[s - 1])

            copy.start()

    sum_send(0)

    for c in turn_copies:
        c.wait_recv()
    up_full = [up_own[:, k].reshape(rank, key_width) for k in range(own_blocks)]
    for k in range(own_blocks):
        value = dot(up_full[k], cot[me * own_blocks + k], NT)
        rank_grad[me * own_blocks + k] = (adapter_scale * value).astype(rank_grad.dtype)
    grad_copies = [
        remote(rank_grad.at[chunk(me)], rank_grad.at[chunk(me)], {"tensor": p}) for p in others
    ]
    for c in grad_copies:
        c.start()

    def pass_on(i):
        copy_a[i].wait_recv()
        copy_c[i].start()
        copy_d[i].start()

    pass_on(0)
    for c in grad_copies:
        c.wait_recv()

    term_copies = []
    for i, p in enumerate((jx, jd, js, job)):
        for s in range(SLOT_CAP):
            index, valid = slot(p, s)
            live = lax.broadcasted_iota(jnp.int32, (1, BLOCK), 1) < (
                fill_ref[base + index] * valid
            )
            rows = jnp.where(live, rank_grad[index].astype(jnp.float32), 0.0).astype(
                rank_grad.dtype
            )
            term_send[i, s] = jnp.dot(
                rows, tokens[index], preferred_element_type=jnp.float32
            ).astype(term_send.dtype)
        if i < 3:
            c = remote(term_send.at[i], got_terms.at[i], {"job": p})
            c.start()
            term_copies.append(c)
        if i == 1:
            pass_on(1)
            copy_c[0].wait_recv()
            copy_e[0].start()

    gather_recv(1)
    gather_send(2)
    sum_send(1)
    copy_c[1].wait_recv()
    copy_e[1].start()
    down_load.wait()
    copy_b.wait_recv()
    for c in copy_d + copy_e:
        c.wait_recv()

    for b in range(blocks):
        value = dot(down_all[adapter[b]], tokens[b], NT)
        rank_part[b // own_blocks, b % own_blocks] = jnp.where(live_row(b), value, 0.0).astype(
            rank_part.dtype
        )
    rank_copies = [remote(rank_part.at[p], rank_in.at[me], {"tensor": p}) for p in others]
    for c in rank_copies:
        c.start()

    def weights_of(p):
        count = jnp.int32(0)
        index = [jnp.int32(-1)] * SLOT_CAP
        for b in range(blocks):
            hit = jnp.where(owner_ref[p * blocks + b] == job, 1, 0)
            for k in range(SLOT_CAP):
                here = hit * jnp.where(count == k, 1, 0)
                index[k] = index[k] + here * (local_ref[p * blocks + b] + 1)
            count = count + hit
        return [
            [jnp.where(index[k] == a, 1.0, 0.0) for k in range(SLOT_CAP)] for a in range(adapters)
        ]

    lanes = 128

    def take_terms(got, p, first):
        weights = weights_of(p)

        @pl.loop(0, width // lanes)
        def _(t):
            columns = pl.ds(pl.multiple_of(t * lanes, lanes), lanes)
            values = [got[k, :, columns].astype(jnp.float32) for k in range(SLOT_CAP)]
            for a in range(adapters):
                total = None if first else down_total[a, :, columns]
                for k in range(SLOT_CAP):
                    term = weights[a][k] * values[k]
                    total = term if total is None else total + term
                down_total[a, :, columns] = total

    take_terms(term_send.at[3], job, True)
    term_copies[2].wait_recv()
    take_terms(got_terms.at[2], js, False)

    gather_recv(2)
    sum_send(2)
    out_copies = []
    tile_out = 512

    def token_chunk(z):
        @pl.loop(0, width // tile_out)
        def _(t):
            columns = pl.ds(pl.multiple_of(t * tile_out, tile_out), tile_out)
            rows = cot[pl.ds(z * own_blocks, own_blocks)].reshape(own_blocks * BLOCK, key_width)
            acc = dot(rows, weight[columns, :], NT)
            for k in range(own_blocks):
                b = z * own_blocks + k
                value = acc[k * BLOCK : (k + 1) * BLOCK] + dot(
                    rank_grad[b], down_all[adapter[b], :, columns], TN
                )
                staged[b, :, columns] = jnp.where(live_column(b), value, 0.0).astype(staged.dtype)

        out_copies.append(
            load(
                staged.at[pl.ds(z * own_blocks, own_blocks)],
                grad_tokens_out.at[pl.ds(z * own_blocks, own_blocks)],
            )
        )

    for z in range(n // 2):
        token_chunk(z)

    for c in rank_copies:
        c.wait_recv()
    rank_in[me] = rank_part[me]
    rank_sum = jnp.sum(rank_in[...].astype(jnp.float32), axis=0)
    rank_sum = rank_sum.astype(jnp.bfloat16)
    for t in range(n):
        rank_split[t] = rank_sum[:, t * portion : (t + 1) * portion]
    mine_copies = [remote(rank_split.at[p], rank_mine.at[chunk(me)], {"tensor": p}) for p in others]
    for c in mine_copies:
        c.start()
    for k in range(own_blocks):
        rank_mine[me * own_blocks + k] = rank_split[me, k]

    for z in range(n // 2, n):
        token_chunk(z)

    for c in mine_copies:
        c.wait_recv()
    up_term_copies = []
    for i, p in enumerate((jx, jd, js, job)):
        for s in range(SLOT_CAP):
            index, valid = slot(p, s)
            value = jnp.dot(rank_mine[index], cot[index], preferred_element_type=jnp.float32)
            up_term_send[i, s] = (
                jnp.where(valid > 0, adapter_scale, 0.0) * value
            ).astype(up_term_send.dtype)
        if i < 3:
            c = remote(up_term_send.at[i], got_up_terms.at[i], {"job": p})
            c.start()
            up_term_copies.append(c)

    term_copies[0].wait_recv()
    take_terms(got_terms.at[0], jx, False)

    @pl.when(me >= 1)
    def _():
        right_sum[n - 2][1].wait_recv()

    @pl.when(me <= n - 2)
    def _():
        left_sum[n - 2][1].wait_recv()

    for k in range(own_blocks):
        value = part[me * own_blocks + k].astype(jnp.float32) + adapter_scale * dot(
            rank_sum[k], up_own[:, k].reshape(rank, key_width), TN
        )
        value = value + jnp.where(me >= 1, from_left[n - 2, k].astype(jnp.float32), 0.0)
        value = value + jnp.where(me <= n - 2, from_right[n - 2, k].astype(jnp.float32), 0.0)
        projected_ref[pl.ds(k * BLOCK, BLOCK), :] = value.astype(projected_ref.dtype)

    term_copies[1].wait_recv()
    take_terms(got_terms.at[1], jd, False)
    down_out = load(down_total, grad_down_out)
    for c in up_term_copies:
        c.wait_recv()
    sources = [(got_up_terms.at[i], p) for i, p in enumerate((jx, jd, js))]
    sources.append((up_term_send.at[3], job))
    tables = [weights_of(p) for _, p in sources]
    for a in range(adapters):
        total = jnp.zeros((portion, key_width), jnp.float32)
        for (got, _), table in zip(sources, tables):
            for k in range(SLOT_CAP):
                total = total + table[a][k] * got[k].astype(jnp.float32)
        grad_up_out[a] = total
    for c in (
        up_copies
        + copy_a
        + [copy_b]
        + copy_c
        + copy_d
        + copy_e
        + turn_copies
        + grad_copies
        + term_copies
        + rank_copies
        + mine_copies
        + up_term_copies
    ):
        c.wait_send()
    for s in range(n - 1):

        @pl.when((me >= s) & (me <= n - 2))
        def _(s=s):
            right_gather[s].wait_send()

        @pl.when((me <= n - 1 - s) & (me >= 1))
        def _(s=s):
            left_gather[s].wait_send()

        @pl.when((me <= s) & (me <= n - 2))
        def _(s=s):
            right_sum[s][1].wait_send()

        @pl.when((n - 1 - me <= s) & (me >= 1))
        def _(s=s):
            left_sum[s][1].wait_send()

    down_out.wait()
    for c in out_copies:
        c.wait()


def local(
    tokens,
    frozen_key_weight,
    adapter_down_maps,
    adapter_up_maps,
    cotangent,
    block_owner_job,
    block_local_adapter,
    block_live_rows,
):
    own_rows, key_width = cotangent.shape
    n = lax.axis_size("tensor")
    jobs = lax.axis_size("job")
    adapters, width, rank = adapter_down_maps.shape
    portion = adapter_up_maps.shape[1]
    fits = own_rows % BLOCK == 0 and n == 4 and jobs == 4
    if not (fits and lax.axis_size("groups") == 2 and adapters % 4 == 0 and portion == 16):
        return general(
            tokens,
            frozen_key_weight,
            adapter_down_maps,
            adapter_up_maps,
            cotangent,
            block_owner_job,
            block_local_adapter,
            block_live_rows,
        )
    row_total = tokens.shape[0]
    blocks = row_total // BLOCK
    own_blocks = own_rows // BLOCK
    owners = block_owner_job.reshape(-1)
    bf16 = jnp.bfloat16
    vmem = pl.BlockSpec(memory_space=pltpu.VMEM)
    hbm = pl.BlockSpec(memory_space=pl.ANY)
    smem = pl.BlockSpec(memory_space=pltpu.SMEM)
    copies = 8 * (n - 1) + 18
    projected, grad_tokens, grad_down, grad_up = pl.pallas_call(
        functools.partial(main_kernel, n),
        in_specs=[smem, smem, smem, hbm, hbm, hbm, hbm, hbm],
        out_specs=[vmem, hbm, hbm, vmem],
        out_shape=[
            jax.ShapeDtypeStruct((own_rows, key_width), bf16),
            jax.ShapeDtypeStruct((blocks, BLOCK, width), bf16),
            jax.ShapeDtypeStruct((adapters, rank, width), jnp.float32),
            jax.ShapeDtypeStruct((adapters, portion, key_width), jnp.float32),
        ],
        scratch_shapes=[
            pltpu.VMEM((blocks, BLOCK, width), bf16),
            pltpu.VMEM(frozen_key_weight.shape, bf16),
            pltpu.VMEM((jobs * adapters, rank, width), bf16),
            pltpu.VMEM((jobs * adapters, portion, key_width), bf16),
            pltpu.VMEM((blocks, BLOCK, key_width), bf16),
            pltpu.VMEM((blocks, BLOCK, key_width), bf16),
            pltpu.VMEM((n - 1, own_blocks, BLOCK, key_width), bf16),
            pltpu.VMEM((n - 1, own_blocks, BLOCK, key_width), bf16),
            pltpu.VMEM((n, own_blocks, portion, key_width), bf16),
            pltpu.VMEM((n, own_blocks, portion, key_width), bf16),
            pltpu.VMEM((blocks, rank, BLOCK), bf16),
            pltpu.VMEM((n, own_blocks, rank, BLOCK), bf16),
            pltpu.VMEM((n, own_blocks, rank, BLOCK), bf16),
            pltpu.VMEM((n, own_blocks, portion, BLOCK), bf16),
            pltpu.VMEM((blocks, portion, BLOCK), bf16),
            pltpu.VMEM((jobs, SLOT_CAP, rank, width), bf16),
            pltpu.VMEM((jobs, SLOT_CAP, portion, key_width), bf16),
            pltpu.VMEM((blocks, BLOCK, width), bf16),
            pltpu.VMEM((jobs - 1, SLOT_CAP, rank, width), bf16),
            pltpu.VMEM((jobs - 1, SLOT_CAP, portion, key_width), bf16),
            pltpu.VMEM((adapters, rank, width), jnp.float32),
            pltpu.SemaphoreType.DMA((6 + n,)),
            pltpu.SemaphoreType.DMA((copies,)),
            pltpu.SemaphoreType.DMA((copies,)),
        ],
        compiler_params=pltpu.CompilerParams(
            collective_id=0, has_side_effects=True, vmem_limit_bytes=60 * 1024 * 1024
        ),
        cost_estimate=pl.CostEstimate(
            flops=4 * row_total * width * key_width,
            bytes_accessed=4 * row_total * width,
            transcendentals=0,
        ),
        name="project_and_grads",
    )(
        owners,
        block_local_adapter,
        block_live_rows,
        tokens.reshape(blocks, BLOCK, width),
        frozen_key_weight,
        jnp.transpose(adapter_down_maps, (0, 2, 1)),
        adapter_up_maps,
        cotangent.reshape(own_blocks, BLOCK, key_width),
    )
    return (
        projected,
        grad_tokens.reshape(row_total, width),
        jnp.transpose(grad_down, (0, 2, 1)),
        grad_up,
    )


def solution(mesh):
    placed = (
        P(("groups", "job"), "tensor"),
        P("tensor", None),
        P("job", "tensor", None),
        P("job", "tensor", None),
        P(("groups", "job", "tensor"), None),
        P("groups", None),
        P("groups"),
        P("groups"),
    )
    return jax.shard_map(
        local,
        mesh=mesh,
        in_specs=placed,
        out_specs=(
            P(("groups", "job", "tensor"), None),
            P(("groups", "job"), "tensor"),
            P(("groups", "job"), "tensor", None),
            P(("groups", "job"), "tensor", None),
        ),
        check_vma=False,
    )
```
